1024 devices in a mesh: replica: 64 (over x, z_lo), fsdp: 16 (over y, z_hi, core).
Axes of the slice: x: 4, y: 4, z: 32 (z_hi: 2, z_lo: 16; z = z_hi * 16 + z_lo), core: 2. Of those that a mesh axis runs over, the one named last changes fastest.
Arguments:
- local_weights: bfloat16 [64, 256, 8192], P('replica', 'fsdp'), may hold values from -16 to 16
- base_weights: float32 [256, 8192], P('fsdp'), may hold values from -6 to 6
- momentum: float32 [256, 8192], P('fsdp', 'replica'), may hold values from -6 to 6
Outputs:
- merged_fragment: bfloat16 [64, 256, 8192], P('replica')
- new_base: float32 [256, 8192], P('fsdp', 'replica')
- new_momentum: float32 [256, 8192], P('fsdp', 'replica')
The draws below stay inside these ranges and needn't reach their ends.
All inputs are finite; a program needn't handle non-finite values.
Results may differ from the reference program's by a relative error of at most 0.0055.
Values may be sent and summed in bfloat16 or wider, within the bound.
A program may use at most 32 MiB of HBM per device.

```python
import jax
import jax.numpy as jnp
from jax import lax

D = 8192
BLOCK = 32
ROWS = 256
N_REPLICA = 64


def strengthened(entries, rng, source, target, parts, factor):
    owner, partner = [(jnp.arange(entries.shape[dim]) // (entries.shape[dim] // parts)).reshape([-1 if axis == dim else 1 for axis in range(entries.ndim)]) for dim in (source, target)]
    chosen = jax.random.permutation(rng, parts)[partner]
    strong = (owner == chosen) | (owner == (partner + parts // 2) % parts)
    return jnp.where(strong, factor * entries, entries)


def block_scale(stream_key, dims, split, least, high):
    gain = 1.0
    for position, parts in split:
        heights = jax.random.uniform(jax.random.fold_in(jax.random.fold_in(stream_key, 6), position), (parts,), jnp.float32, least / len(split), high / len(split))
        gain = gain * jnp.repeat(jnp.exp(heights), dims[position] // parts).reshape((-1,) + (1,) * (len(dims) - 1 - position))
    return gain


def noise(rng, extent, scale, most, shards=(), held_as=jnp.bfloat16):
    array = jax.random.normal(rng, extent, jnp.float32) * scale
    if len(shards) > 0:
        array = block_scale(rng, extent, shards, -0.22, 0.18) * array
    return jnp.clip(array, min=-most, max=most).astype(held_as)


def noise_with(stream_key, dims, deviation, most, split, heavy, held_as=jnp.bfloat16):
    result = deviation * jax.random.normal(stream_key, dims, jnp.float32)
    if split:
        result = result * block_scale(stream_key, dims, split, -0.22, 0.18)
    return jnp.clip(strengthened(result, jax.random.fold_in(stream_key, 3), *heavy), -most, most).astype(held_as)


def setup_inputs(seed: int = 0) -> dict:
    splits = jax.random.split(jax.random.key(seed), 4)
    return {
        "local_weights": noise_with(splits[0], (N_REPLICA, ROWS, D), 1.0, 16.0, ((0, 64), (1, 16)), (0, 2, 64, 4.0)),
        "base_weights": noise(splits[1], (ROWS, D), 1.0, 6.0, ((0, 16),), jnp.float32),
        "momentum": noise(splits[2], (ROWS, D), 1.0, 6.0, ((0, 16), (1, 64)), jnp.float32),
    }


def encode(delta):
    rows = delta.shape[0]
    blocks = delta.reshape(rows, D // BLOCK, BLOCK)
    largest = jnp.max(jnp.abs(blocks), axis=2)
    scale = (jnp.maximum(largest, 1.0) / 6.0).astype(jnp.bfloat16)
    ratio = blocks / scale.astype(jnp.float32)[:, :, None]
    codes = jnp.clip(ratio, -4.0, 4.0).astype(jnp.bfloat16)
    return codes, scale


def decode(codes, scale):
    rows = codes.shape[0]
    values = codes.astype(jnp.float32) * scale.astype(jnp.float32)[:, :, None]
    return values.reshape(rows, D)


def reference(local_weights, base_weights, momentum):
    def accumulate(total, local_one):
        delta = base_weights - local_one.astype(jnp.float32)
        codes, scale = encode(delta)
        return total + decode(codes, scale), None

    total, unused = lax.scan(accumulate, jnp.zeros((ROWS, D), jnp.float32), local_weights)
    grad = total / N_REPLICA
    new_momentum = 0.9 * momentum + grad
    new_base = base_weights - 0.7 * (grad + 0.9 * new_momentum)

    def blend(local_one):
        return (0.5 * new_base + 0.5 * local_one.astype(jnp.float32)).astype(jnp.bfloat16)

    merged_fragment = lax.map(blend, local_weights)
    return merged_fragment, new_base, new_momentum
```

```python
import jax
import jax.numpy as jnp
from jax import lax
from jax.experimental import pallas as pl
from jax.experimental.pallas import tpu as pltpu
from jax.sharding import PartitionSpec as P

MESH = pl.DeviceIdType.MESH
T = 128
BLOCK = 32


def kernel(
    local, base, mom, out, new_base, new_mom,
    dec, rx, p1, rb, p2, ra, nbh, nbbuf, zbuf,
    bulk_s, bulk_r, red_s, red_r, gat_s, gat_r, y_s, y_r, sib_s, sib_r,
):
    rep, fs = lax.axis_index("replica"), lax.axis_index("fsdp")
    x, zl = rep // 16, rep % 16
    a, b = zl // 4, zl % 4
    y, zh, core = fs // 4, (fs // 2) % 2, fs % 2

    def at_x(d):
        return (((x + d) % 4) * 16 + zl, fs)

    def at_a(d):
        return (x * 16 + ((a + d) % 4) * 4 + b, fs)

    def at_b(d):
        return (x * 16 + a * 4 + (b + d) % 4, fs)

    def at_y(d):
        return (rep, ((y + d) % 4) * 4 + zh * 2 + core)

    half = (rep, y * 4 + (1 - zh) * 2 + core)
    sibling = (rep, y * 4 + zh * 2 + (1 - core))

    barrier = pltpu.get_barrier_semaphore()
    peers = [f(d) for f in (at_x, at_a, at_b, at_y) for d in (1, 2, 3)]
    for peer in peers + [half, sibling]:
        pl.semaphore_signal(barrier, inc=1, device_id=peer, device_id_type=MESH)

    lane = lax.broadcasted_iota(jnp.int32, (16, T), 1)
    upper = [(lane // s) % 2 == 1 for s in (1, 2, 4, 8, 16)]

    def encode(q, carry):
        for i in range(4):
            for j in range(4):
                cols = pl.ds(pl.multiple_of(q * 2048 + (i * 4 + j) * T, T), T)
                delta = base[:, cols] - local[:, cols].astype(jnp.float32)
                most = jnp.abs(delta)
                for k, s in enumerate((1, 2, 4, 8, 16)):
                    other = jnp.where(
                        upper[k], pltpu.roll(most, s, 1), pltpu.roll(most, T - s, 1)
                    )
                    most = jnp.maximum(most, other)
                scale = (jnp.maximum(most, 1.0) / 6.0).astype(jnp.bfloat16)
                bound = 4.0 * scale.astype(jnp.float32)
                dec[q, j, i] = jnp.clip(delta, -bound, bound).astype(jnp.bfloat16)
        return carry

    lax.fori_loop(0, 4, encode, 0)
    pl.semaphore_wait(barrier, 14)

    def remote(src, dst, s, r, to):
        copy = pltpu.make_async_remote_copy(
            src_ref=src, dst_ref=dst, send_sem=s, recv_sem=r,
            device_id=to, device_id_type=MESH,
        )
        copy.start()
        return copy

    sent = []

    def exchange(copies):
        for copy in copies:
            copy.wait_recv()
        sent.extend(copies)

    x_copies = [
        remote(dec.at[(x + d) % 4], rx.at[d - 1], red_s.at[d - 1], red_r.at[d - 1], at_x(d))
        for d in (1, 2, 3)
    ]
    bulk = []
    for q in range(4):
        cols = pl.ds(pl.multiple_of(((x + q) % 4) * 2048, 2048), 2048)
        bulk.append(remote(local.at[:, cols], zbuf.at[:, cols], bulk_s.at[q], bulk_r.at[q], half))
    exchange(x_copies)

    def sum_x(j, carry):
        for i in range(4):
            total = dec[x, j, i].astype(jnp.float32)
            for d in range(3):
                total = total + rx[d, j, i].astype(jnp.float32)
            p1[j, i] = total.astype(jnp.bfloat16)
        return carry

    lax.fori_loop(0, 4, sum_x, 0)
    exchange([
        remote(p1.at[(b + d) % 4], rb.at[d - 1], red_s.at[2 + d], red_r.at[2 + d], at_b(d))
        for d in (1, 2, 3)
    ])
    for i in range(4):
        total = p1[b, i].astype(jnp.float32)
        for d in range(3):
            total = total + rb[d, i].astype(jnp.float32)
        p2[i] = total.astype(jnp.bfloat16)
    exchange([
        remote(p2.at[(a + d) % 4], ra.at[d - 1], red_s.at[5 + d], red_r.at[5 + d], at_a(d))
        for d in (1, 2, 3)
    ])
    total = p2[a].astype(jnp.float32)
    for d in range(3):
        total = total + ra[d].astype(jnp.float32)
    grad = total / 64.0
    momentum = 0.9 * mom[...] + grad
    own = base[:, pl.ds(pl.multiple_of(rep * T, T), T)]
    updated = own - 0.7 * (grad + 0.9 * momentum)
    new_mom[...] = momentum
    new_base[...] = updated
    nbh[...] = updated.astype(jnp.bfloat16)
    nbbuf[x, b, a, zh] = updated.astype(jnp.bfloat16)

    exchange([remote(nbh, nbbuf.at[x, b, a, zh], gat_s.at[0], gat_r.at[0], half)])
    exchange([
        remote(nbbuf.at[x, b, a], nbbuf.at[x, b, a], gat_s.at[d], gat_r.at[d], at_a(d))
        for d in (1, 2, 3)
    ])
    exchange([
        remote(nbbuf.at[x, b], nbbuf.at[x, b], gat_s.at[3 + d], gat_r.at[3 + d], at_b(d))
        for d in (1, 2, 3)
    ])
    x_gather = [
        remote(nbbuf.at[x], nbbuf.at[x], gat_s.at[6 + d], gat_r.at[6 + d], at_x(d))
        for d in (1, 2, 3)
    ]

    def blend(q, rows, which):
        place = y * 4 + which * 2 + core
        for i in range(4):
            for j in range(4):
                cols = pl.ds(pl.multiple_of(q * 2048 + (i * 4 + j) * T, T), T)
                value = 0.5 * nbbuf[q, j, i, which].astype(jnp.float32)
                value = value + 0.5 * rows[:, cols].astype(jnp.float32)
                out[place, :, cols] = value.astype(jnp.bfloat16)

    def block(place, q):
        return out.at[place, :, pl.ds(pl.multiple_of(q * 2048, 2048), 2048)]

    y_copies, sib_copies = {}, {}

    def spread(k, q, n):
        which = zh if k == 0 else 1 - zh
        here = block(y * 4 + which * 2 + core, q)
        for d in (1, 2, 3):
            y_copies[k, n, d] = remote(here, here, y_s.at[k, n, d - 1], y_r.at[k, n, d - 1], at_y(d))
        sib_copies[k, n, 0] = remote(here, here, sib_s.at[k, n, 0], sib_r.at[k, n, 0], sibling)

    def relay(k, q, n):
        which = zh if k == 0 else 1 - zh
        for d in (1, 2, 3):
            y_copies[k, n, d].wait_recv()
            here = block(((y + 4 - d) % 4) * 4 + which * 2 + core, q)
            sib_copies[k, n, d] = remote(here, here, sib_s.at[k, n, d], sib_r.at[k, n, d], sibling)

    order = [(x + 4 - d) % 4 for d in range(4)]
    for n in range(4):
        if n > 0:
            x_gather[n - 1].wait_recv()
        blend(order[n], local, zh)
        spread(0, order[n], n)
    landing = [0, 3, 2, 1]
    for n in range(4):
        bulk[landing[n]].wait_recv()
        blend(order[n], zbuf, 1 - zh)
        spread(1, order[n], n)
        relay(0, order[n], n)
    for n in range(4):
        relay(1, order[n], n)
    for k in range(2):
        for n in range(4):
            for d in range(4):
                sib_copies[k, n, d].wait()
            for d in (1, 2, 3):
                y_copies[k, n, d].wait_send()
    for copy in sent + bulk + x_gather:
        copy.wait_send()


def per_device(local_weights, base_weights, momentum):
    bf16, dma = jnp.bfloat16, pltpu.SemaphoreType.DMA
    vmem = pl.BlockSpec(memory_space=pltpu.VMEM)
    merged, new_base, new_momentum = pl.pallas_call(
        kernel,
        out_shape=(
            jax.ShapeDtypeStruct((16, 16, 8192), bf16),
            jax.ShapeDtypeStruct((16, T), jnp.float32),
            jax.ShapeDtypeStruct((16, T), jnp.float32),
        ),
        in_specs=[vmem] * 3,
        out_specs=(vmem,) * 3,
        scratch_shapes=[
            pltpu.VMEM((4, 4, 4, 16, T), bf16),
            pltpu.VMEM((3, 4, 4, 16, T), bf16),
            pltpu.VMEM((4, 4, 16, T), bf16),
            pltpu.VMEM((3, 4, 16, T), bf16),
            pltpu.VMEM((4, 16, T), bf16),
            pltpu.VMEM((3, 16, T), bf16),
            pltpu.VMEM((16, T), bf16),
            pltpu.VMEM((4, 4, 4, 2, 16, T), bf16),
            pltpu.VMEM((16, 8192), bf16),
            dma((4,)), dma((4,)), dma((9,)), dma((9,)), dma((10,)), dma((10,)),
            dma((2, 4, 3)), dma((2, 4, 3)), dma((2, 4, 4)), dma((2, 4, 4)),
        ],
        compiler_params=pltpu.CompilerParams(
            collective_id=0, has_side_effects=True, vmem_limit_bytes=24 * 2**20
        ),
    )(local_weights[0], base_weights, momentum)
    return merged.reshape(1, 256, 8192), new_base, new_momentum


def solution(mesh):
    in_specs = (P("replica", "fsdp", None), P("fsdp", None), P("fsdp", "replica"))
    out_specs = (P("replica", None, None), P("fsdp", "replica"), P("fsdp", "replica"))
    return jax.shard_map(
        per_device, mesh=mesh, in_specs=in_specs, out_specs=out_specs, check_vma=False
    )
```

```python
import jax
import jax.numpy as jnp
from jax import lax
from jax.experimental import pallas as pl
from jax.experimental.pallas import tpu as pltpu
from jax.sharding import PartitionSpec as P

MESH = pl.DeviceIdType.MESH
T = 128
LEG = 4
CUT = ((0, 1), (2, 3), (0, 1), (2, 3))


def kernel(
    local, base, mom, out, new_base, new_mom,
    dec, rx, p1, rb, p2, ra, nbh, mine, theirs, ring,
    ring_s, ring_r, red_s, red_r, gat_s, gat_r, far_s, far_r, y_s, y_r, sib_s, sib_r, known,
):
    rep, fs = lax.axis_index("replica"), lax.axis_index("fsdp")
    x, zl = rep // 16, rep % 16
    a, b = zl // 4, zl % 4
    y, zh, core = fs // 4, (fs // 2) % 2, fs % 2

    def at_x(d):
        return (((x + d) % 4) * 16 + zl, fs)

    def at_a(d):
        return (x * 16 + ((a + d) % 4) * 4 + b, fs)

    def at_b(d):
        return (x * 16 + a * 4 + (b + d) % 4, fs)

    def at_y(d):
        return (rep, ((y + d) % 4) * 4 + zh * 2 + core)

    def far(d):
        return (x * 16 + ((a + d) % 4) * 4 + b, y * 4 + (1 - zh) * 2 + core)

    def along(d):
        z = (zh * 16 + zl + 32 + (LEG if d == 0 else -LEG)) % 32
        return (x * 16 + z % 16, y * 4 + (z // 16) * 2 + core)

    sibling = (rep, y * 4 + zh * 2 + (1 - core))

    barrier = pltpu.get_barrier_semaphore()
    peers = [f(d) for f in (at_x, at_b, at_y) for d in (1, 2, 3)] + [along(0), along(1), sibling]
    for peer in peers:
        pl.semaphore_signal(barrier, inc=1, device_id=peer, device_id_type=MESH)

    lane = lax.broadcasted_iota(jnp.int32, (16, T), 1)
    upper = [(lane // s) % 2 == 1 for s in (1, 2, 4, 8, 16)]

    def encode(q, carry):
        for i in range(4):
            for j in range(4):
                cols = pl.ds(pl.multiple_of(q * 2048 + (i * 4 + j) * T, T), T)
                delta = base[:, cols] - local[:, cols].astype(jnp.float32)
                most = jnp.abs(delta)
                for k, s in enumerate((1, 2, 4, 8, 16)):
                    other = jnp.where(
                        upper[k], pltpu.roll(most, s, 1), pltpu.roll(most, T - s, 1)
                    )
                    most = jnp.maximum(most, other)
                scale = (jnp.maximum(most, 1.0) / 6.0).astype(jnp.bfloat16)
                bound = 4.0 * scale.astype(jnp.float32)
                dec[q, j, i] = jnp.clip(delta, -bound, bound).astype(jnp.bfloat16)
        return carry

    lax.fori_loop(0, 4, encode, 0)
    pl.semaphore_wait(barrier, 12)

    def remote(src, dst, s, r, to):
        copy = pltpu.make_async_remote_copy(
            src_ref=src, dst_ref=dst, send_sem=s, recv_sem=r,
            device_id=to, device_id_type=MESH,
        )
        copy.start()
        return copy

    sent = []

    def arrived(copies):
        for copy in copies:
            copy.wait_recv()
        sent.extend(copies)

    def tell(n):
        for d in (0, 1):
            pl.semaphore_signal(known.at[n], inc=1, device_id=along(d), device_id_type=MESH)

    order = [(x + 4 - d) % 4 for d in range(4)]
    legs = {}

    def forward(k, c):
        for d in (0, 1):
            if k == 0:
                source = local.at[:, pl.ds(pl.multiple_of(order[c] * 2048 + d * 1024, 1024), 1024)]
            else:
                legs[k - 1, d, c].wait_recv()
                source = ring.at[k - 1, d, c]
            legs[k, d, c] = remote(source, ring.at[k, d, c], ring_s.at[k, d, c], ring_r.at[k, d, c], along(d))

    copies = [
        remote(dec.at[(x + d) % 4], rx.at[d - 1], red_s.at[d - 1], red_r.at[d - 1], at_x(d))
        for d in (1, 2, 3)
    ]
    for c in range(4):
        forward(0, c)
    tell(0)
    arrived(copies)

    def sum_x(j, carry):
        for i in range(4):
            total = dec[x, j, i].astype(jnp.float32)
            for d in range(3):
                total = total + rx[d, j, i].astype(jnp.float32)
            p1[j, i] = total.astype(jnp.bfloat16)
        return carry

    lax.fori_loop(0, 4, sum_x, 0)
    copies = [
        remote(p1.at[(b + d) % 4], rb.at[d - 1], red_s.at[2 + d], red_r.at[2 + d], at_b(d))
        for d in (1, 2, 3)
    ]
    pl.semaphore_wait(known.at[0], 2)
    tell(1)
    arrived(copies)
    for i in range(4):
        total = p1[b, i].astype(jnp.float32)
        for d in range(3):
            total = total + rb[d, i].astype(jnp.float32)
        p2[i] = total.astype(jnp.bfloat16)
    pl.semaphore_wait(known.at[1], 2)
    tell(2)
    copies = [
        remote(p2.at[(a + d) % 4], ra.at[d - 1], red_s.at[5 + d], red_r.at[5 + d], at_a(d))
        for d in (1, 2, 3)
    ]
    for c in CUT[0]:
        forward(1, c)
    pl.semaphore_wait(known.at[2], 2)
    arrived(copies)
    total = p2[a].astype(jnp.float32)
    for d in range(3):
        total = total + ra[d].astype(jnp.float32)
    grad = total / 64.0
    momentum = 0.9 * mom[...] + grad
    own = base[:, pl.ds(pl.multiple_of(rep * T, T), T)]
    updated = own - 0.7 * (grad + 0.9 * momentum)
    new_mom[...] = momentum
    new_base[...] = updated
    nbh[...] = updated.astype(jnp.bfloat16)

    near_a = [remote(nbh, mine.at[x, b, a], gat_s.at[d - 1], gat_r.at[d - 1], at_a(d)) for d in (1, 2, 3)]
    far_a = [remote(nbh, theirs.at[x, b, a], far_s.at[6 + d], far_r.at[6 + d], far(d)) for d in range(4)]
    mine[x, b, a] = updated.astype(jnp.bfloat16)
    for c in CUT[1]:
        forward(1, c)
    arrived(near_a)

    def to_b(which, s, r):
        return [remote(which.at[x, b], which.at[x, b], s.at[d - 1], r.at[d - 1], at_b(d)) for d in (1, 2, 3)]

    def to_x(which, s, r):
        return [remote(which.at[x], which.at[x], s.at[2 + d], r.at[2 + d], at_x(d)) for d in (1, 2, 3)]

    near_b = to_b(mine, gat_s.at[pl.ds(3, 6)], gat_r.at[pl.ds(3, 6)])
    for c in CUT[2]:
        forward(2, c)
    arrived(far_a)
    far_b = to_b(theirs, far_s, far_r)
    arrived(near_b)
    near_x = to_x(mine, gat_s.at[pl.ds(3, 6)], gat_r.at[pl.ds(3, 6)])
    for c in CUT[3]:
        forward(2, c)
    arrived(far_b)
    far_x = to_x(theirs, far_s, far_r)

    def blend(which, q, i, rows, cols, place, at):
        for j in range(4):
            value = 0.5 * which[q, j, i].astype(jnp.float32)
            value = value + 0.5 * rows[:, cols(j)].astype(jnp.float32)
            out[place, :, pl.ds(pl.multiple_of(at + j * T, T), T)] = value.astype(jnp.bfloat16)

    y_copies, sib_copies = {}, {}

    def spread(m, which, at, wide):
        here = out.at[y * 4 + which * 2 + core, :, pl.ds(pl.multiple_of(at, 1024), wide)]
        for d in (1, 2, 3):
            y_copies[m, d] = remote(here, here, y_s.at[m, d - 1], y_r.at[m, d - 1], at_y(d))
        sib_copies[m, 0] = remote(here, here, sib_s.at[m, 0], sib_r.at[m, 0], sibling)

    def relay(m, which, at, wide):
        for d in (1, 2, 3):
            y_copies[m, d].wait_recv()
            place = ((y + 4 - d) % 4) * 4 + which * 2 + core
            here = out.at[place, :, pl.ds(pl.multiple_of(at, 1024), wide)]
            sib_copies[m, d] = remote(here, here, sib_s.at[m, d], sib_r.at[m, d], sibling)

    for n in range(4):
        if n > 0:
            near_x[n - 1].wait_recv()
        at = order[n] * 2048
        for i in range(4):
            blend(
                mine, order[n], i, local,
                lambda j: pl.ds(pl.multiple_of(at + (i * 4 + j) * T, T), T),
                y * 4 + zh * 2 + core, at + i * 512,
            )
        spread(n, zh, at, 2048)
        forward(3, n)
    for n in range(4):
        if n > 0:
            far_x[n - 1].wait_recv()
        for d in (0, 1):
            legs[3, d, n].wait_recv()
            at = order[n] * 2048 + d * 1024
            for i in (0, 1):
                blend(
                    theirs, order[n], d * 2 + i, ring.at[3, d, n],
                    lambda j: pl.ds((i * 4 + j) * T, T),
                    y * 4 + (1 - zh) * 2 + core, at + i * 512,
                )
            spread(4 + n * 2 + d, 1 - zh, at, 1024)
        relay(n, zh, order[n] * 2048, 2048)
    for n in range(4):
        for d in (0, 1):
            relay(4 + n * 2 + d, 1 - zh, order[n] * 2048 + d * 1024, 1024)
    for copy in sib_copies.values():
        copy.wait()
    for copy in [*y_copies.values(), *legs.values(), *sent, *near_x, *far_x]:
        copy.wait_send()


def per_device(local_weights, base_weights, momentum):
    bf16, dma = jnp.bfloat16, pltpu.SemaphoreType.DMA
    vmem = pl.BlockSpec(memory_space=pltpu.VMEM)
    merged, new_base, new_momentum = pl.pallas_call(
        kernel,
        out_shape=(
            jax.ShapeDtypeStruct((16, 16, 8192), bf16),
            jax.ShapeDtypeStruct((16, T), jnp.float32),
            jax.ShapeDtypeStruct((16, T), jnp.float32),
        ),
        in_specs=[vmem] * 3,
        out_specs=(vmem,) * 3,
        scratch_shapes=[
            pltpu.VMEM((4, 4, 4, 16, T), bf16),
            pltpu.VMEM((3, 4, 4, 16, T), bf16),
            pltpu.VMEM((4, 4, 16, T), bf16),
            pltpu.VMEM((3, 4, 16, T), bf16),
            pltpu.VMEM((4, 16, T), bf16),
            pltpu.VMEM((3, 16, T), bf16),
            pltpu.VMEM((16, T), bf16),
            pltpu.VMEM((4, 4, 4, 16, T), bf16),
            pltpu.VMEM((4, 4, 4, 16, T), bf16),
            pltpu.VMEM((4, 2, 4, 16, 1024), bf16),
            dma((4, 2, 4)), dma((4, 2, 4)), dma((9,)), dma((9,)), dma((9,)), dma((9,)), dma((10,)), dma((10,)),
            dma((12, 3)), dma((12, 3)), dma((12, 4)), dma((12, 4)), pltpu.SemaphoreType.REGULAR((3,)),
        ],
        compiler_params=pltpu.CompilerParams(
            collective_id=0, has_side_effects=True, vmem_limit_bytes=24 * 2**20
        ),
    )(local_weights[0], base_weights, momentum)
    return merged.reshape(1, 256, 8192), new_base, new_momentum


def solution(mesh):
    in_specs = (P("replica", "fsdp", None), P("fsdp", None), P("fsdp", "replica"))
    out_specs = (P("replica", None, None), P("fsdp", "replica"), P("fsdp", "replica"))
    return jax.shard_map(
        per_device, mesh=mesh, in_specs=in_specs, out_specs=out_specs, check_vma=False
    )
```

```python
import jax
import jax.numpy as jnp
from jax import lax
from jax.experimental import pallas as pl
from jax.experimental.pallas import tpu as pltpu
from jax.sharding import PartitionSpec as P

MESH = pl.DeviceIdType.MESH
T = 128
LEG = 2
LEGS = 16 // LEG
PLAN = (
    "1.0", "1.1", "x", "1.2", "1.3", "b", "2.0", "2.1", "2.2", "2.3", "3.0", "3.1", "a", "3.2", "3.3", "4.0",
    "4.1", "na", "4.2", "4.3", "5.0", "fa", "5.1", "nb", "5.2", "5.3", "fb", "6.0", "m0", "6.1", "m1", "6.2",
    "6.3", "m2", "7.0", "m3", "7.1", "7.2", "7.3",
)
STRAIGHT = 12


def kernel(
    local_h, base_h, mom_h, out, new_base, new_mom,
    local, base, mom, in_sem,
    dec, rx, p1, rb, p2, ra, nbh, mine, theirs, ring,
    ring_s, ring_r, red_s, red_r, gat_s, gat_r, far_s, far_r, y_s, y_r, sib_s, sib_r, known,
):
    rep, fs = lax.axis_index("replica"), lax.axis_index("fsdp")
    x, zl = rep // 16, rep % 16
    a, b = zl // 4, zl % 4
    y, zh, core = fs // 4, (fs // 2) % 2, fs % 2

    def at_x(d):
        return (((x + d) % 4) * 16 + zl, fs)

    def at_a(d):
        return (x * 16 + ((a + d) % 4) * 4 + b, fs)

    def at_b(d):
        return (x * 16 + a * 4 + (b + d) % 4, fs)

    def at_y(d, which=core):
        return (rep, ((y + d) % 4) * 4 + zh * 2 + which)

    def far(d):
        return (x * 16 + ((a + d) % 4) * 4 + b, y * 4 + (1 - zh) * 2 + core)

    def along(d, n):
        z = (zh * 16 + zl + 32 + (n if d == 0 else -n)) % 32
        return (x * 16 + z % 16, y * 4 + (z // 16) * 2 + core)

    sibling = (rep, y * 4 + zh * 2 + (1 - core))

    barrier = pltpu.get_barrier_semaphore()
    peers = [f(d) for f in (at_x, at_b, at_y) for d in (1, 2, 3)] + [along(d, n) for d in (0, 1) for n in {LEG, 4}] + [sibling]
    peers = peers + [at_y(d, 1 - core) for d in (1, 2, 3)]
    for peer in peers:
        pl.semaphore_signal(barrier, inc=1, device_id=peer, device_id_type=MESH)

    loads = [
        pltpu.make_async_copy(source, target, in_sem.at[n])
        for n, (source, target) in enumerate(((base_h, base), (local_h, local), (mom_h, mom)))
    ]
    for load in loads:
        load.start()
    for load in loads:
        load.wait()

    lane = lax.broadcasted_iota(jnp.int32, (16, T), 1)
    upper = [(lane // s) % 2 == 1 for s in (1, 2, 4, 8, 16)]

    def encode(q, carry):
        for i in range(4):
            for j in range(4):
                cols = pl.ds(pl.multiple_of(q * 2048 + (i * 4 + j) * T, T), T)
                delta = base[:, cols] - local[:, cols].astype(jnp.float32)
                most = jnp.abs(delta)
                for k, s in enumerate((1, 2, 4, 8, 16)):
                    other = jnp.where(
                        upper[k], pltpu.roll(most, s, 1), pltpu.roll(most, T - s, 1)
                    )
                    most = jnp.maximum(most, other)
                scale = (jnp.maximum(most, 1.0) / 6.0).astype(jnp.bfloat16)
                bound = 4.0 * scale.astype(jnp.float32)
                dec[q, j, i] = jnp.clip(delta, -bound, bound).astype(jnp.bfloat16)
        return carry

    lax.fori_loop(0, 4, encode, 0)
    pl.semaphore_wait(barrier, len(peers))

    def remote(src, dst, s, r, to):
        copy = pltpu.make_async_remote_copy(
            src_ref=src, dst_ref=dst, send_sem=s, recv_sem=r,
            device_id=to, device_id_type=MESH,
        )
        copy.start()
        return copy

    sent = []

    def arrived(copies):
        for copy in copies:
            copy.wait_recv()
        sent.extend(copies)

    def tell(n):
        for d in (0, 1):
            pl.semaphore_signal(known.at[n], inc=1, device_id=along(d, 4), device_id_type=MESH)

    order = [(x + 4 - d) % 4 for d in range(4)]
    legs = {}

    def forward(k, c):
        for d in (0, 1):
            if k == 0:
                source = local.at[:, pl.ds(pl.multiple_of(order[c] * 2048 + d * 1024, 1024), 1024)]
            else:
                legs[k - 1, d, c].wait_recv()
                source = ring.at[k - 1, d, c]
            legs[k, d, c] = remote(source, ring.at[k, d, c], ring_s.at[k, d, c], ring_r.at[k, d, c], along(d, LEG))

    copies = [
        remote(dec.at[(x + d) % 4], rx.at[d - 1], red_s.at[d - 1], red_r.at[d - 1], at_x(d))
        for d in (1, 2, 3)
    ]
    for c in range(4):
        forward(0, c)
    tell(0)

    def sum_x(j, carry):
        for i in range(4):
            total = dec[x, j, i].astype(jnp.float32)
            for d in range(3):
                total = total + rx[d, j, i].astype(jnp.float32)
            p1[j, i] = total.astype(jnp.bfloat16)
        return carry

    def to_b(which, s, r):
        return [remote(which.at[x, b], which.at[x, b], s.at[d - 1], r.at[d - 1], at_b(d)) for d in (1, 2, 3)]

    def to_x(which, s, r):
        return [remote(which.at[x], which.at[x], s.at[2 + d], r.at[2 + d], at_x(d)) for d in (1, 2, 3)]

    def blend(which, q, i, rows, cols, place, at):
        for j in range(4):
            value = 0.5 * which[q, j, i].astype(jnp.float32)
            value = value + 0.5 * rows[:, cols(j)].astype(jnp.float32)
            out[place, :, pl.ds(pl.multiple_of(at + j * T, T), T)] = value.astype(jnp.bfloat16)

    y_copies, sib_copies = {}, {}

    def straight(m):
        return m >= STRAIGHT

    def spread(m, which, at, wide):
        here = out.at[y * 4 + which * 2 + core, :, pl.ds(pl.multiple_of(at, 1024), wide)]
        for d in (1, 2, 3):
            y_copies[m, d] = remote(here, here, y_s.at[m, d - 1], y_r.at[m, d - 1], at_y(d))
        if straight(m):
            for d in (1, 2, 3):
                sib_copies[m, d] = remote(here, here, sib_s.at[m, d], sib_r.at[m, d], at_y(d, 1 - core))
        sib_copies[m, 0] = remote(here, here, sib_s.at[m, 0], sib_r.at[m, 0], sibling)

    def relay(m, which, at, wide):
        for d in (1, 2, 3):
            y_copies[m, d].wait_recv()
            if straight(m):
                continue
            place = ((y + 4 - d) % 4) * 4 + which * 2 + core
            here = out.at[place, :, pl.ds(pl.multiple_of(at, 1024), wide)]
            sib_copies[m, d] = remote(here, here, sib_s.at[m, d], sib_r.at[m, d], sibling)

    def blend_mine(n, near_x):
        if n > 0:
            near_x[n - 1].wait_recv()
        at = order[n] * 2048
        for i in range(4):
            blend(
                mine, order[n], i, local,
                lambda j: pl.ds(pl.multiple_of(at + (i * 4 + j) * T, T), T),
                y * 4 + zh * 2 + core, at + i * 512,
            )
        spread(n, zh, at, 2048)

    def step_x(copies):
        arrived(copies)
        lax.fori_loop(0, 4, sum_x, 0)
        copies = [
            remote(p1.at[(b + d) % 4], rb.at[d - 1], red_s.at[2 + d], red_r.at[2 + d], at_b(d))
            for d in (1, 2, 3)
        ]
        pl.semaphore_wait(known.at[0], 2)
        tell(1)
        return copies

    def step_b(copies):
        arrived(copies)
        for i in range(4):
            total = p1[b, i].astype(jnp.float32)
            for d in range(3):
                total = total + rb[d, i].astype(jnp.float32)
            p2[i] = total.astype(jnp.bfloat16)
        pl.semaphore_wait(known.at[1], 2)
        tell(2)
        return [
            remote(p2.at[(a + d) % 4], ra.at[d - 1], red_s.at[5 + d], red_r.at[5 + d], at_a(d))
            for d in (1, 2, 3)
        ]

    def step_a(copies):
        pl.semaphore_wait(known.at[2], 2)
        arrived(copies)
        total = p2[a].astype(jnp.float32)
        for d in range(3):
            total = total + ra[d].astype(jnp.float32)
        grad = total / 64.0
        momentum = 0.9 * mom[...] + grad
        own = base[:, pl.ds(pl.multiple_of(rep * T, T), T)]
        updated = own - 0.7 * (grad + 0.9 * momentum)
        nbh[...] = updated.astype(jnp.bfloat16)
        near = [remote(nbh, mine.at[x, b, a], gat_s.at[d - 1], gat_r.at[d - 1], at_a(d)) for d in (1, 2, 3)]
        other = [remote(nbh, theirs.at[x, b, a], far_s.at[6 + d], far_r.at[6 + d], far(d)) for d in range(4)]
        mine[x, b, a] = updated.astype(jnp.bfloat16)
        new_mom[...] = momentum
        new_base[...] = updated
        return near, other

    at = {"x": copies}
    for step in PLAN:
        if step == "x":
            at["b"] = step_x(at["x"])
        elif step == "b":
            at["a"] = step_b(at["b"])
        elif step == "a":
            at["na"], at["fa"] = step_a(at["a"])
        elif step == "na":
            arrived(at["na"])
            at["nb"] = to_b(mine, gat_s.at[pl.ds(3, 6)], gat_r.at[pl.ds(3, 6)])
        elif step == "fa":
            arrived(at["fa"])
            at["fb"] = to_b(theirs, far_s, far_r)
        elif step == "nb":
            arrived(at["nb"])
            near_x = to_x(mine, gat_s.at[pl.ds(3, 6)], gat_r.at[pl.ds(3, 6)])
        elif step == "fb":
            arrived(at["fb"])
            far_x = to_x(theirs, far_s, far_r)
        elif step[0] == "m":
            blend_mine(int(step[1]), near_x)
        else:
            k, c = step.split(".")
            forward(int(k), int(c))
    for n in range(4):
        if n > 0:
            far_x[n - 1].wait_recv()
        for d in (0, 1):
            legs[LEGS - 1, d, n].wait_recv()
            at = order[n] * 2048 + d * 1024
            for i in (0, 1):
                blend(
                    theirs, order[n], d * 2 + i, ring.at[LEGS - 1, d, n],
                    lambda j: pl.ds((i * 4 + j) * T, T),
                    y * 4 + (1 - zh) * 2 + core, at + i * 512,
                )
            spread(4 + n * 2 + d, 1 - zh, at, 1024)
        relay(n, zh, order[n] * 2048, 2048)
    for n in range(4):
        for d in (0, 1):
            relay(4 + n * 2 + d, 1 - zh, order[n] * 2048 + d * 1024, 1024)
    for copy in sib_copies.values():
        copy.wait()
    for copy in [*y_copies.values(), *legs.values(), *sent, *near_x, *far_x]:
        copy.wait_send()


def per_device(local_weights, base_weights, momentum):
    bf16, dma = jnp.bfloat16, pltpu.SemaphoreType.DMA
    vmem = pl.BlockSpec(memory_space=pltpu.VMEM)
    merged, new_base, new_momentum = pl.pallas_call(
        kernel,
        out_shape=(
            jax.ShapeDtypeStruct((16, 16, 8192), bf16),
            jax.ShapeDtypeStruct((16, T), jnp.float32),
            jax.ShapeDtypeStruct((16, T), jnp.float32),
        ),
        in_specs=[pl.BlockSpec(memory_space=pltpu.HBM)] * 3,
        out_specs=(vmem,) * 3,
        scratch_shapes=[
            pltpu.VMEM((16, 8192), bf16), pltpu.VMEM((16, 8192), jnp.float32), pltpu.VMEM((16, T), jnp.float32), dma((3,)),
            pltpu.VMEM((4, 4, 4, 16, T), bf16),
            pltpu.VMEM((3, 4, 4, 16, T), bf16),
            pltpu.VMEM((4, 4, 16, T), bf16),
            pltpu.VMEM((3, 4, 16, T), bf16),
            pltpu.VMEM((4, 16, T), bf16),
            pltpu.VMEM((3, 16, T), bf16),
            pltpu.VMEM((16, T), bf16),
            pltpu.VMEM((4, 4, 4, 16, T), bf16),
            pltpu.VMEM((4, 4, 4, 16, T), bf16),
            pltpu.VMEM((LEGS, 2, 4, 16, 1024), bf16),
            dma((LEGS, 2, 4)), dma((LEGS, 2, 4)), dma((9,)), dma((9,)), dma((9,)), dma((9,)), dma((10,)), dma((10,)),
            dma((12, 3)), dma((12, 3)), dma((12, 4)), dma((12, 4)), pltpu.SemaphoreType.REGULAR((3,)),
        ],
        compiler_params=pltpu.CompilerParams(
            collective_id=0, has_side_effects=True, vmem_limit_bytes=24 * 2**20
        ),
    )(*(pltpu.with_memory_space_constraint(v, pltpu.HBM) for v in (local_weights[0], base_weights, momentum)))
    return merged.reshape(1, 256, 8192), new_base, new_momentum


def solution(mesh):
    in_specs = (P("replica", "fsdp", None), P("fsdp", None), P("fsdp", "replica"))
    out_specs = (P("replica", None, None), P("fsdp", "replica"), P("fsdp", "replica"))
    return jax.shard_map(
        per_device, mesh=mesh, in_specs=in_specs, out_specs=out_specs, check_vma=False
    )
```

```python
import jax
import jax.numpy as jnp
from jax import lax
from jax.experimental import pallas as pl
from jax.experimental.pallas import tpu as pltpu
from jax.sharding import PartitionSpec as P

MESH = pl.DeviceIdType.MESH
T = 128
LEG = 2
LEGS = 16 // LEG
PLAN = (
    "1.0", "1.1", "x", "1.2", "1.3", "b", "2.0", "2.1", "2.2", "2.3", "3.0", "3.1", "a", "3.2", "3.3", "4.0",
    "4.1", "na", "4.2", "4.3", "5.0", "fa", "5.1", "nb", "5.2", "5.3", "fb", "6.0", "m0", "m1", "m2", "m3", "6.1",
    "6.2", "6.3", "7.0", "7.1", "7.2", "7.3",
)
STRAIGHT = 12


def kernel(
    local_h, base_h, mom_h, out, new_base, new_mom,
    local, base, mom, in_sem,
    dec, rx, p1, rb, p2, ra, nbh, mine, theirs, ring,
    ring_s, ring_r, red_s, red_r, gat_s, gat_r, far_s, far_r, y_s, y_r, sib_s, sib_r, known,
):
    rep, fs = lax.axis_index("replica"), lax.axis_index("fsdp")
    x, zl = rep // 16, rep % 16
    a, b = zl // 4, zl % 4
    y, zh, core = fs // 4, (fs // 2) % 2, fs % 2

    def at_x(d):
        return (((x + d) % 4) * 16 + zl, fs)

    def at_a(d):
        return (x * 16 + ((a + d) % 4) * 4 + b, fs)

    def at_b(d):
        return (x * 16 + a * 4 + (b + d) % 4, fs)

    def at_y(d, which=core):
        return (rep, ((y + d) % 4) * 4 + zh * 2 + which)

    def far(d):
        return (x * 16 + ((a + d) % 4) * 4 + b, y * 4 + (1 - zh) * 2 + core)

    def along(d, n):
        z = (zh * 16 + zl + 32 + (n if d == 0 else -n)) % 32
        return (x * 16 + z % 16, y * 4 + (z // 16) * 2 + core)

    sibling = (rep, y * 4 + zh * 2 + (1 - core))

    barrier = pltpu.get_barrier_semaphore()
    peers = [f(d) for f in (at_x, at_b, at_y) for d in (1, 2, 3)] + [along(d, n) for d in (0, 1) for n in {LEG, 4}] + [sibling]
    peers = peers + [at_y(d, 1 - core) for d in (1, 2, 3)]
    for peer in peers:
        pl.semaphore_signal(barrier, inc=1, device_id=peer, device_id_type=MESH)

    loads = [
        pltpu.make_async_copy(source, target, in_sem.at[n])
        for n, (source, target) in enumerate(((base_h, base), (local_h, local), (mom_h, mom)))
    ]
    for load in loads:
        load.start()
    for load in loads:
        load.wait()

    lane = lax.broadcasted_iota(jnp.int32, (16, T), 1)
    upper = [(lane // s) % 2 == 1 for s in (1, 2, 4, 8, 16)]

    def encode(q, carry):
        for i in range(4):
            for j in range(4):
                cols = pl.ds(pl.multiple_of(q * 2048 + (i * 4 + j) * T, T), T)
                delta = base[:, cols] - local[:, cols].astype(jnp.float32)
                most = jnp.abs(delta)
                for k, s in enumerate((1, 2, 4, 8, 16)):
                    other = jnp.where(
                        upper[k], pltpu.roll(most, s, 1), pltpu.roll(most, T - s, 1)
                    )
                    most = jnp.maximum(most, other)
                scale = (jnp.maximum(most, 1.0) / 6.0).astype(jnp.bfloat16)
                bound = 4.0 * scale.astype(jnp.float32)
                dec[q, j, i] = jnp.clip(delta, -bound, bound).astype(jnp.bfloat16)
        return carry

    lax.fori_loop(0, 4, encode, 0)
    pl.semaphore_wait(barrier, len(peers))

    def remote(src, dst, s, r, to):
        copy = pltpu.make_async_remote_copy(
            src_ref=src, dst_ref=dst, send_sem=s, recv_sem=r,
            device_id=to, device_id_type=MESH,
        )
        copy.start()
        return copy

    sent = []

    def arrived(copies):
        for copy in copies:
            copy.wait_recv()
        sent.extend(copies)

    def tell(n):
        for d in (0, 1):
            pl.semaphore_signal(known.at[n], inc=1, device_id=along(d, 4), device_id_type=MESH)

    order = [(x + 4 - d) % 4 for d in range(4)]
    legs = {}

    def forward(k, c):
        for d in (0, 1):
            if k == 0:
                source = local.at[:, pl.ds(pl.multiple_of(order[c] * 2048 + d * 1024, 1024), 1024)]
            else:
                legs[k - 1, d, c].wait_recv()
                source = ring.at[k - 1, d, c]
            legs[k, d, c] = remote(source, ring.at[k, d, c], ring_s.at[k, d, c], ring_r.at[k, d, c], along(d, LEG))

    copies = [
        remote(dec.at[(x + d) % 4], rx.at[d - 1], red_s.at[d - 1], red_r.at[d - 1], at_x(d))
        for d in (1, 2, 3)
    ]
    for c in range(4):
        forward(0, c)
    tell(0)

    def sum_x(j, carry):
        for i in range(4):
            total = dec[x, j, i].astype(jnp.float32)
            for d in range(3):
                total = total + rx[d, j, i].astype(jnp.float32)
            p1[j, i] = total.astype(jnp.bfloat16)
        return carry

    def to_b(which, s, r):
        return [remote(which.at[x, b], which.at[x, b], s.at[d - 1], r.at[d - 1], at_b(d)) for d in (1, 2, 3)]

    def to_x(which, s, r):
        return [remote(which.at[x], which.at[x], s.at[2 + d], r.at[2 + d], at_x(d)) for d in (1, 2, 3)]

    def blend(which, q, i, rows, cols, place, at):
        for j in range(4):
            value = 0.5 * which[q, j, i].astype(jnp.float32)
            value = value + 0.5 * rows[:, cols(j)].astype(jnp.float32)
            out[place, :, pl.ds(pl.multiple_of(at + j * T, T), T)] = value.astype(jnp.bfloat16)

    y_copies, sib_copies = {}, {}

    def straight(m):
        return m >= STRAIGHT

    def spread(m, which, at, wide):
        here = out.at[y * 4 + which * 2 + core, :, pl.ds(pl.multiple_of(at, 1024), wide)]
        for d in (1, 2, 3):
            y_copies[m, d] = remote(here, here, y_s.at[m, d - 1], y_r.at[m, d - 1], at_y(d))
        if straight(m):
            for d in (1, 2, 3):
                sib_copies[m, d] = remote(here, here, sib_s.at[m, d], sib_r.at[m, d], at_y(d, 1 - core))
        sib_copies[m, 0] = remote(here, here, sib_s.at[m, 0], sib_r.at[m, 0], sibling)

    def relay(m, which, at, wide):
        for d in (1, 2, 3):
            y_copies[m, d].wait_recv()
            if straight(m):
                continue
            place = ((y + 4 - d) % 4) * 4 + which * 2 + core
            here = out.at[place, :, pl.ds(pl.multiple_of(at, 1024), wide)]
            sib_copies[m, d] = remote(here, here, sib_s.at[m, d], sib_r.at[m, d], sibling)

    def blend_mine(n, near_x):
        if n > 0:
            near_x[n - 1].wait_recv()
        at = order[n] * 2048
        for i in range(4):
            blend(
                mine, order[n], i, local,
                lambda j: pl.ds(pl.multiple_of(at + (i * 4 + j) * T, T), T),
                y * 4 + zh * 2 + core, at + i * 512,
            )
        spread(n, zh, at, 2048)

    def step_x(copies):
        arrived(copies)
        lax.fori_loop(0, 4, sum_x, 0)
        copies = [
            remote(p1.at[(b + d) % 4], rb.at[d - 1], red_s.at[2 + d], red_r.at[2 + d], at_b(d))
            for d in (1, 2, 3)
        ]
        pl.semaphore_wait(known.at[0], 2)
        tell(1)
        return copies

    def step_b(copies):
        arrived(copies)
        for i in range(4):
            total = p1[b, i].astype(jnp.float32)
            for d in range(3):
                total = total + rb[d, i].astype(jnp.float32)
            p2[i] = total.astype(jnp.bfloat16)
        pl.semaphore_wait(known.at[1], 2)
        tell(2)
        return [
            remote(p2.at[(a + d) % 4], ra.at[d - 1], red_s.at[5 + d], red_r.at[5 + d], at_a(d))
            for d in (1, 2, 3)
        ]

    def step_a(copies):
        pl.semaphore_wait(known.at[2], 2)
        arrived(copies)
        total = p2[a].astype(jnp.float32)
        for d in range(3):
            total = total + ra[d].astype(jnp.float32)
        grad = total / 64.0
        momentum = 0.9 * mom[...] + grad
        own = base[:, pl.ds(pl.multiple_of(rep * T, T), T)]
        updated = own - 0.7 * (grad + 0.9 * momentum)
        nbh[...] = updated.astype(jnp.bfloat16)
        near = [remote(nbh, mine.at[x, b, a], gat_s.at[d - 1], gat_r.at[d - 1], at_a(d)) for d in (1, 2, 3)]
        other = [remote(nbh, theirs.at[x, b, a], far_s.at[6 + d], far_r.at[6 + d], far(d)) for d in range(4)]
        mine[x, b, a] = updated.astype(jnp.bfloat16)
        new_mom[...] = momentum
        new_base[...] = updated
        return near, other

    at = {"x": copies}
    for step in PLAN:
        if step == "x":
            at["b"] = step_x(at["x"])
        elif step == "b":
            at["a"] = step_b(at["b"])
        elif step == "a":
            at["na"], at["fa"] = step_a(at["a"])
        elif step == "na":
            arrived(at["na"])
            at["nb"] = to_b(mine, gat_s.at[pl.ds(3, 6)], gat_r.at[pl.ds(3, 6)])
        elif step == "fa":
            arrived(at["fa"])
            at["fb"] = to_b(theirs, far_s, far_r)
        elif step == "nb":
            arrived(at["nb"])
            near_x = to_x(mine, gat_s.at[pl.ds(3, 6)], gat_r.at[pl.ds(3, 6)])
        elif step == "fb":
            arrived(at["fb"])
            far_x = to_x(theirs, far_s, far_r)
        elif step[0] == "m":
            blend_mine(int(step[1]), near_x)
        else:
            k, c = step.split(".")
            forward(int(k), int(c))
    for n in range(4):
        if n > 0:
            far_x[n - 1].wait_recv()
        for d in (0, 1):
            legs[LEGS - 1, d, n].wait_recv()
            at = order[n] * 2048 + d * 1024
            for i in (0, 1):
                blend(
                    theirs, order[n], d * 2 + i, ring.at[LEGS - 1, d, n],
                    lambda j: pl.ds((i * 4 + j) * T, T),
                    y * 4 + (1 - zh) * 2 + core, at + i * 512,
                )
            spread(4 + n * 2 + d, 1 - zh, at, 1024)
        if n > 0:
            relay(n - 1, zh, order[n - 1] * 2048, 2048)
    relay(3, zh, order[3] * 2048, 2048)
    for n in range(4):
        for d in (0, 1):
            relay(4 + n * 2 + d, 1 - zh, order[n] * 2048 + d * 1024, 1024)
    for copy in sib_copies.values():
        copy.wait()
    for copy in [*y_copies.values(), *legs.values(), *sent, *near_x, *far_x]:
        copy.wait_send()


def per_device(local_weights, base_weights, momentum):
    bf16, dma = jnp.bfloat16, pltpu.SemaphoreType.DMA
    vmem = pl.BlockSpec(memory_space=pltpu.VMEM)
    merged, new_base, new_momentum = pl.pallas_call(
        kernel,
        out_shape=(
            jax.ShapeDtypeStruct((16, 16, 8192), bf16),
            jax.ShapeDtypeStruct((16, T), jnp.float32),
            jax.ShapeDtypeStruct((16, T), jnp.float32),
        ),
        in_specs=[pl.BlockSpec(memory_space=pltpu.HBM)] * 3,
        out_specs=(vmem,) * 3,
        scratch_shapes=[
            pltpu.VMEM((16, 8192), bf16), pltpu.VMEM((16, 8192), jnp.float32), pltpu.VMEM((16, T), jnp.float32), dma((3,)),
            pltpu.VMEM((4, 4, 4, 16, T), bf16),
            pltpu.VMEM((3, 4, 4, 16, T), bf16),
            pltpu.VMEM((4, 4, 16, T), bf16),
            pltpu.VMEM((3, 4, 16, T), bf16),
            pltpu.VMEM((4, 16, T), bf16),
            pltpu.VMEM((3, 16, T), bf16),
            pltpu.VMEM((16, T), bf16),
            pltpu.VMEM((4, 4, 4, 16, T), bf16),
            pltpu.VMEM((4, 4, 4, 16, T), bf16),
            pltpu.VMEM((LEGS, 2, 4, 16, 1024), bf16),
            dma((LEGS, 2, 4)), dma((LEGS, 2, 4)), dma((9,)), dma((9,)), dma((9,)), dma((9,)), dma((10,)), dma((10,)),
            dma((12, 3)), dma((12, 3)), dma((12, 4)), dma((12, 4)), pltpu.SemaphoreType.REGULAR((3,)),
        ],
        compiler_params=pltpu.CompilerParams(
            collective_id=0, has_side_effects=True, vmem_limit_bytes=24 * 2**20
        ),
    )(*(pltpu.with_memory_space_constraint(v, pltpu.HBM) for v in (local_weights[0], base_weights, momentum)))
    return merged.reshape(1, 256, 8192), new_base, new_momentum


def solution(mesh):
    in_specs = (P("replica", "fsdp", None), P("fsdp", None), P("fsdp", "replica"))
    out_specs = (P("replica", None, None), P("fsdp", "replica"), P("fsdp", "replica"))
    return jax.shard_map(
        per_device, mesh=mesh, in_specs=in_specs, out_specs=out_specs, check_vma=False
    )
```

```python
import jax
import jax.numpy as jnp
from jax import lax
from jax.experimental import pallas as pl
from jax.experimental.pallas import tpu as pltpu
from jax.sharding import PartitionSpec as P

MESH = pl.DeviceIdType.MESH
T = 128
LEG = 2
LEGS = 16 // LEG
PLAN = (
    "1.0", "1.1", "x", "1.2", "1.3", "b", "2.0", "2.1", "2.2", "2.3", "3.0", "3.1", "a", "3.2", "3.3", "4.0",
    "4.1", "na", "4.2", "4.3", "5.0", "fa", "5.1", "nb", "5.2", "5.3", "fb", "6.0", "m0", "m1", "m2", "m3", "6.1",
    "6.2", "6.3", "7.0", "7.1", "7.2", "7.3",
)
STRAIGHT = 12


def kernel(
    local_h, base_h, mom_h, out, new_base, new_mom,
    local, base, mom, in_sem,
    dec, rx, p1, rb, p2, ra, nbh, mine, theirs, ring,
    ring_s, ring_r, red_s, red_r, gat_s, gat_r, far_s, far_r, y_s, y_r, sib_s, sib_r, known,
):
    rep, fs = lax.axis_index("replica"), lax.axis_index("fsdp")
    x, zl = rep // 16, rep % 16
    a, b = zl // 4, zl % 4
    y, zh, core = fs // 4, (fs // 2) % 2, fs % 2

    def at_x(d):
        return (((x + d) % 4) * 16 + zl, fs)

    def at_a(d):
        return (x * 16 + ((a + d) % 4) * 4 + b, fs)

    def at_b(d):
        return (x * 16 + a * 4 + (b + d) % 4, fs)

    def at_y(d, which=core):
        return (rep, ((y + d) % 4) * 4 + zh * 2 + which)

    def far(d):
        return (x * 16 + ((a + d) % 4) * 4 + b, y * 4 + (1 - zh) * 2 + core)

    def along(d, n):
        z = (zh * 16 + zl + 32 + (n if d == 0 else -n)) % 32
        return (x * 16 + z % 16, y * 4 + (z // 16) * 2 + core)

    sibling = (rep, y * 4 + zh * 2 + (1 - core))

    barrier = pltpu.get_barrier_semaphore()
    peers = [f(d) for f in (at_x, at_b, at_y) for d in (1, 2, 3)] + [along(d, n) for d in (0, 1) for n in {LEG, 4}] + [sibling]
    peers = peers + [at_y(d, 1 - core) for d in (1, 2, 3)]
    for peer in peers:
        pl.semaphore_signal(barrier, inc=1, device_id=peer, device_id_type=MESH)

    loads = [
        pltpu.make_async_copy(source, target, in_sem.at[n])
        for n, (source, target) in enumerate(((base_h, base), (local_h, local), (mom_h, mom)))
    ]
    for load in loads:
        load.start()
    for load in loads:
        load.wait()

    lane = lax.broadcasted_iota(jnp.int32, (16, T), 1)
    upper = [(lane // s) % 2 == 1 for s in (1, 2, 4, 8, 16)]

    def encode(q, carry):
        for i in range(4):
            for j in range(4):
                cols = pl.ds(pl.multiple_of(q * 2048 + (i * 4 + j) * T, T), T)
                delta = base[:, cols] - local[:, cols].astype(jnp.float32)
                most = jnp.abs(delta)
                for k, s in enumerate((1, 2, 4, 8, 16)):
                    other = jnp.where(
                        upper[k], pltpu.roll(most, s, 1), pltpu.roll(most, T - s, 1)
                    )
                    most = jnp.maximum(most, other)
                scale = (jnp.maximum(most, 1.0) / 6.0).astype(jnp.bfloat16)
                bound = 4.0 * scale.astype(jnp.float32)
                dec[q, j, i] = jnp.clip(delta, -bound, bound).astype(jnp.bfloat16)
        return carry

    lax.fori_loop(0, 4, encode, 0)
    pl.semaphore_wait(barrier, len(peers))

    def remote(src, dst, s, r, to):
        copy = pltpu.make_async_remote_copy(
            src_ref=src, dst_ref=dst, send_sem=s, recv_sem=r,
            device_id=to, device_id_type=MESH,
        )
        copy.start()
        return copy

    sent = []

    def arrived(copies):
        for copy in copies:
            copy.wait_recv()
        sent.extend(copies)

    def tell(n):
        for d in (0, 1):
            pl.semaphore_signal(known.at[n], inc=1, device_id=along(d, 4), device_id_type=MESH)

    order = [(x + 4 - d) % 4 for d in range(4)]
    legs = {}

    def forward(k, c):
        for d in (0, 1):
            if k == 0:
                source = local.at[:, pl.ds(pl.multiple_of(order[c] * 2048 + d * 1024, 1024), 1024)]
            else:
                legs[k - 1, d, c].wait_recv()
                source = ring.at[k - 1, d, c]
            legs[k, d, c] = remote(source, ring.at[k, d, c], ring_s.at[k, d, c], ring_r.at[k, d, c], along(d, LEG))

    copies = [
        remote(dec.at[(x + d) % 4], rx.at[d - 1], red_s.at[d - 1], red_r.at[d - 1], at_x(d))
        for d in (1, 2, 3)
    ]
    for c in range(4):
        forward(0, c)
    tell(0)

    def sum_x(j, carry):
        for i in range(4):
            total = dec[x, j, i].astype(jnp.float32)
            for d in range(3):
                total = total + rx[d, j, i].astype(jnp.float32)
            p1[j, i] = total.astype(jnp.bfloat16)
        return carry

    def to_b(which, s, r):
        return [remote(which.at[x, b], which.at[x, b], s.at[d - 1], r.at[d - 1], at_b(d)) for d in (1, 2, 3)]

    def to_x(which, s, r):
        return [remote(which.at[x], which.at[x], s.at[2 + d], r.at[2 + d], at_x(d)) for d in (1, 2, 3)]

    def blend(which, q, i, rows, cols, place, at):
        for j in range(4):
            value = 0.5 * which[q, j, i].astype(jnp.float32)
            value = value + 0.5 * rows[:, cols(j)].astype(jnp.float32)
            out[place, :, pl.ds(pl.multiple_of(at + j * T, T), T)] = value.astype(jnp.bfloat16)

    y_copies, sib_copies = {}, {}

    def straight(m):
        return m >= STRAIGHT

    def spread(m, which, at, wide):
        here = out.at[y * 4 + which * 2 + core, :, pl.ds(pl.multiple_of(at, 1024), wide)]
        for d in (1, 2, 3):
            y_copies[m, d] = remote(here, here, y_s.at[m, d - 1], y_r.at[m, d - 1], at_y(d))
        if straight(m):
            for d in (1, 2, 3):
                sib_copies[m, d] = remote(here, here, sib_s.at[m, d], sib_r.at[m, d], at_y(d, 1 - core))
        sib_copies[m, 0] = remote(here, here, sib_s.at[m, 0], sib_r.at[m, 0], sibling)

    def relay(m, which, at, wide):
        for d in (1, 2, 3):
            y_copies[m, d].wait_recv()
            if straight(m):
                continue
            place = ((y + 4 - d) % 4) * 4 + which * 2 + core
            here = out.at[place, :, pl.ds(pl.multiple_of(at, 1024), wide)]
            sib_copies[m, d] = remote(here, here, sib_s.at[m, d], sib_r.at[m, d], sibling)

    def blend_mine(n, near_x):
        if n > 0:
            near_x[n - 1].wait_recv()
        at = order[n] * 2048
        for i in range(4):
            blend(
                mine, order[n], i, local,
                lambda j: pl.ds(pl.multiple_of(at + (i * 4 + j) * T, T), T),
                y * 4 + zh * 2 + core, at + i * 512,
            )
        spread(n, zh, at, 2048)

    def step_x(copies):
        arrived(copies)
        lax.fori_loop(0, 4, sum_x, 0)
        copies = [
            remote(p1.at[(b + d) % 4], rb.at[d - 1], red_s.at[2 + d], red_r.at[2 + d], at_b(d))
            for d in (1, 2, 3)
        ]
        pl.semaphore_wait(known.at[0], 2)
        tell(1)
        return copies

    def step_b(copies):
        arrived(copies)
        for i in range(4):
            total = p1[b, i].astype(jnp.float32)
            for d in range(3):
                total = total + rb[d, i].astype(jnp.float32)
            p2[i] = total.astype(jnp.bfloat16)
        pl.semaphore_wait(known.at[1], 2)
        tell(2)
        return [
            remote(p2.at[(a + d) % 4], ra.at[d - 1], red_s.at[5 + d], red_r.at[5 + d], at_a(d))
            for d in (1, 2, 3)
        ]

    def step_a(copies):
        pl.semaphore_wait(known.at[2], 2)
        arrived(copies)
        total = p2[a].astype(jnp.float32)
        for d in range(3):
            total = total + ra[d].astype(jnp.float32)
        grad = total / 64.0
        momentum = 0.9 * mom[...] + grad
        own = base[:, pl.ds(pl.multiple_of(rep * T, T), T)]
        updated = own - 0.7 * (grad + 0.9 * momentum)
        nbh[...] = updated.astype(jnp.bfloat16)
        near = [remote(nbh, mine.at[x, b, a], gat_s.at[d - 1], gat_r.at[d - 1], at_a(d)) for d in (1, 2, 3)]
        other = [remote(nbh, theirs.at[x, b, a], far_s.at[6 + d], far_r.at[6 + d], far(d)) for d in range(4)]
        mine[x, b, a] = updated.astype(jnp.bfloat16)
        new_mom[...] = momentum
        new_base[...] = updated
        return near, other

    at = {"x": copies}
    for step in PLAN:
        if step == "x":
            at["b"] = step_x(at["x"])
        elif step == "b":
            at["a"] = step_b(at["b"])
        elif step == "a":
            at["na"], at["fa"] = step_a(at["a"])
        elif step == "na":
            arrived(at["na"])
            at["nb"] = to_b(mine, gat_s.at[pl.ds(3, 6)], gat_r.at[pl.ds(3, 6)])
        elif step == "fa":
            arrived(at["fa"])
            at["fb"] = to_b(theirs, far_s, far_r)
        elif step == "nb":
            arrived(at["nb"])
            near_x = to_x(mine, gat_s.at[pl.ds(3, 6)], gat_r.at[pl.ds(3, 6)])
        elif step == "fb":
            arrived(at["fb"])
            far_x = to_x(theirs, far_s, far_r)
        elif step[0] == "m":
            blend_mine(int(step[1]), near_x)
        else:
            k, c = step.split(".")
            forward(int(k), int(c))
    for n in range(4):
        if n > 0:
            far_x[n - 1].wait_recv()
        for d in (0, 1):
            legs[LEGS - 1, d, n].wait_recv()
            at = order[n] * 2048 + d * 1024
            for i in (0, 1):
                blend(
                    theirs, order[n], d * 2 + i, ring.at[LEGS - 1, d, n],
                    lambda j: pl.ds((i * 4 + j) * T, T),
                    y * 4 + (1 - zh) * 2 + core, at + i * 512,
                )
            spread(4 + n * 2 + d, 1 - zh, at, 1024)
        if n > 0:
            relay(n - 1, zh, order[n - 1] * 2048, 2048)
        if n > 1:
            for d in (0, 1):
                relay(n * 2 + d, 1 - zh, order[n - 2] * 2048 + d * 1024, 1024)
    relay(3, zh, order[3] * 2048, 2048)
    for n in (2, 3):
        for d in (0, 1):
            relay(4 + n * 2 + d, 1 - zh, order[n] * 2048 + d * 1024, 1024)
    for copy in sib_copies.values():
        copy.wait()
    for copy in [*y_copies.values(), *legs.values(), *sent, *near_x, *far_x]:
        copy.wait_send()


def per_device(local_weights, base_weights, momentum):
    bf16, dma = jnp.bfloat16, pltpu.SemaphoreType.DMA
    vmem = pl.BlockSpec(memory_space=pltpu.VMEM)
    merged, new_base, new_momentum = pl.pallas_call(
        kernel,
        out_shape=(
            jax.ShapeDtypeStruct((16, 16, 8192), bf16),
            jax.ShapeDtypeStruct((16, T), jnp.float32),
            jax.ShapeDtypeStruct((16, T), jnp.float32),
        ),
        in_specs=[pl.BlockSpec(memory_space=pltpu.HBM)] * 3,
        out_specs=(vmem,) * 3,
        scratch_shapes=[
            pltpu.VMEM((16, 8192), bf16), pltpu.VMEM((16, 8192), jnp.float32), pltpu.VMEM((16, T), jnp.float32), dma((3,)),
            pltpu.VMEM((4, 4, 4, 16, T), bf16),
            pltpu.VMEM((3, 4, 4, 16, T), bf16),
            pltpu.VMEM((4, 4, 16, T), bf16),
            pltpu.VMEM((3, 4, 16, T), bf16),
            pltpu.VMEM((4, 16, T), bf16),
            pltpu.VMEM((3, 16, T), bf16),
            pltpu.VMEM((16, T), bf16),
            pltpu.VMEM((4, 4, 4, 16, T), bf16),
            pltpu.VMEM((4, 4, 4, 16, T), bf16),
            pltpu.VMEM((LEGS, 2, 4, 16, 1024), bf16),
            dma((LEGS, 2, 4)), dma((LEGS, 2, 4)), dma((9,)), dma((9,)), dma((9,)), dma((9,)), dma((10,)), dma((10,)),
            dma((12, 3)), dma((12, 3)), dma((12, 4)), dma((12, 4)), pltpu.SemaphoreType.REGULAR((3,)),
        ],
        compiler_params=pltpu.CompilerParams(
            collective_id=0, has_side_effects=True, vmem_limit_bytes=24 * 2**20
        ),
    )(*(pltpu.with_memory_space_constraint(v, pltpu.HBM) for v in (local_weights[0], base_weights, momentum)))
    return merged.reshape(1, 256, 8192), new_base, new_momentum


def solution(mesh):
    in_specs = (P("replica", "fsdp", None), P("fsdp", None), P("fsdp", "replica"))
    out_specs = (P("replica", None, None), P("fsdp", "replica"), P("fsdp", "replica"))
    return jax.shard_map(
        per_device, mesh=mesh, in_specs=in_specs, out_specs=out_specs, check_vma=False
    )
```
